32 devices in a mesh: seg: 4 (over y, x), block: 8 (over z, core).
Axes of the slice: x: 2, y: 2, z: 4, core: 2. Of those that a mesh axis runs over, the one named last changes fastest.
Arguments:
- jacobian: float32 [128, 128, 128], P(('seg', 'block')), may hold values from -2 to 2
- implicit_inv: float32 [128, 128, 128], P(('seg', 'block')), may hold values from -2 to 2, as said below
- input_map: float32 [128, 128, 64], P(('seg', 'block')), may hold values from -0.75 to 0.75
- controls: float32 [128, 64], P(('seg', 'block')), may hold values from -2 to 2
- control_step: float32 [128, 64], P(('seg', 'block')), may hold values from -2 to 2
- state_traj: float32 [128, 128], P(('seg', 'block')), may hold values from -2 to 2
- terminal: float32 [128], replicated, may hold values from -2 to 2
- init_gap: float32 [128], replicated, may hold values from -3 to 3
- counts: int32 [32], P(('seg', 'block')), may hold values from 2 to 4, as said below
Outputs:
- updated: float32 [128, 128], P(('seg', 'block'))
- defect_out: float32 [128, 128], P(('seg', 'block'))
The draws below stay inside these ranges and needn't reach their ends.
Inputs may be any that keep to these rules, and one draw needn't show every extreme that they name: implicit_inv[k] is the inverse of I - jacobian[k] / 2 + jacobian[k] jacobian[k] / 12. `counts`: some block uses all 4 slots and some only half of 4, rounded down; used slots are the first ones of a block.
All inputs are finite; a program needn't handle non-finite values.
Results may differ from the reference program's by a relative error of at most 0.0003.
Values sent between devices are 32-bit elements; how exact they have to be, the bound alone decides.
A program may use at most 64 MiB of HBM per device.

```python
import math
import jax
import jax.numpy as jnp
from jax import lax

NS = 128
NU = 64
KNOTS_DEV = 4
BLOCKS = 32
KNOTS = 128


def dynamics_field(key):
    base_key = jax.random.fold_in(key, 71)
    key_skew, key_damping = jax.random.split(base_key)
    entries = jax.random.normal(key_skew, (KNOTS, NS, NS), jnp.float32)
    skew = 0.5 * (entries - jnp.swapaxes(entries, 1, 2)) / math.sqrt(2.0 * NS)
    damping = jnp.exp(jax.random.uniform(key_damping, (KNOTS, NS), jnp.float32, math.log(0.05), math.log(5.0))) / KNOTS
    return skew - damping[:, :, None] * jnp.eye(NS, dtype=jnp.float32)[None]


def draw_jacobian(key, part):
    return dynamics_field(key)


def draw_implicit_inv(key, part):
    field = dynamics_field(key)
    squared = jnp.einsum('kij,kjl->kil', field, field, precision=lax.Precision.HIGHEST)
    implicit = jnp.eye(NS, dtype=jnp.float32)[None] - 0.5 * field + squared / 12.0
    return jnp.linalg.inv(implicit).astype(jnp.float32)


def draw_counts(key, part):
    base_key = jax.random.fold_in(key, 29)
    values = jax.random.randint(base_key, (BLOCKS,), KNOTS_DEV // 2, KNOTS_DEV + 1)
    order = jax.random.permutation(jax.random.fold_in(base_key, 3), BLOCKS)
    values = values.at[order[0]].set(KNOTS_DEV)
    values = values.at[order[1]].set(KNOTS_DEV // 2)
    return values.astype(jnp.int32)


def shard_levels(key, dims, cuts, smallest, largest):
    factor_of = 1.0
    for dim, blocks in cuts:
        draws = jax.random.uniform(jax.random.fold_in(jax.random.fold_in(key, 6), dim), (blocks,), jnp.float32, smallest / len(cuts), largest / len(cuts))
        factor_of = factor_of * jnp.repeat(jnp.exp(draws), dims[dim] // blocks).reshape((-1,) + (1,) * (len(dims) - 1 - dim))
    return factor_of


def noise(stream_key, extent, spread, reach, cuts=(), kind=jnp.bfloat16):
    values = jax.random.normal(stream_key, extent, jnp.float32) * spread
    if len(cuts) > 0:
        values = shard_levels(stream_key, extent, cuts, -0.22, 0.18) * values
    return jnp.clip(values, min=-reach, max=reach).astype(kind)


def setup_inputs(seed: int = 0) -> dict:
    key_list = jax.random.split(jax.random.key(seed), 10)
    return {
        "jacobian": draw_jacobian(jax.random.fold_in(key_list[9], 71), 0),
        "implicit_inv": draw_implicit_inv(jax.random.fold_in(key_list[9], 71), 0),
        "input_map": noise(key_list[2], (KNOTS, NS, NU), NU ** -0.5, 0.75, ((0, 32),), jnp.float32),
        "controls": noise(key_list[3], (KNOTS, NU), 0.25, 2.0, ((0, 32),), jnp.float32),
        "control_step": noise(key_list[4], (KNOTS, NU), 0.25, 2.0, ((0, 32),), jnp.float32),
        "state_traj": noise(key_list[5], (KNOTS, NS), 0.25, 2.0, ((0, 32),), jnp.float32),
        "terminal": noise(key_list[6], (NS,), 0.25, 2.0, (), jnp.float32),
        "init_gap": noise(key_list[7], (NS,), 0.5, 3.0, (), jnp.float32),
        "counts": draw_counts(jax.random.fold_in(key_list[9], 71), 0),
    }


def matvec(matrix, vector):
    return jnp.dot(matrix, vector, precision=lax.Precision.HIGHEST)

def reference(jacobian, implicit_inv, input_map, controls, control_step, state_traj, terminal, init_gap, counts):
    slot_ids = jnp.arange(KNOTS).astype(jnp.int32)
    device_ids = slot_ids // KNOTS_DEV
    within = slot_ids % KNOTS_DEV
    limits = counts[device_ids]
    active = within < limits
    later_ids = jnp.minimum(slot_ids + 1, KNOTS - 1).astype(jnp.int32)
    first_ids = jnp.minimum((device_ids + 1) * KNOTS_DEV, KNOTS - 1).astype(jnp.int32)
    first_state = jnp.where((device_ids + 1 < BLOCKS)[:, None], state_traj[first_ids], terminal[None])
    next_state = jnp.where((within + 1 < limits)[:, None], state_traj[later_ids], first_state)

    def advance(current, pieces):
        dynamics, inverse, input_mat, control, delta_ctrl, present, upcoming, is_active = pieces
        moved = matvec(dynamics, present)
        explicit_x = present + 0.5 * moved + matvec(dynamics, moved) / 12.0
        moved_next = matvec(dynamics, upcoming)
        implicit_x = upcoming - 0.5 * moved_next + matvec(dynamics, moved_next) / 12.0
        defect = implicit_x - explicit_x - matvec(input_mat, control)
        moved_corr = matvec(dynamics, current)
        explicit_c = current + 0.5 * moved_corr + matvec(dynamics, moved_corr) / 12.0
        fresh_state = matvec(inverse, explicit_c + matvec(input_mat, delta_ctrl) - defect)
        carried = jnp.where(is_active, fresh_state, current)
        result = jnp.where(is_active, upcoming + fresh_state, jnp.zeros_like(upcoming))
        defect_kept = jnp.where(is_active, defect, jnp.zeros_like(defect))
        return (carried, (result, defect_kept))
    _, outputs = lax.scan(advance, init_gap.astype(jnp.float32), (jacobian, implicit_inv, input_map, controls, control_step, state_traj, next_state, active))
    return (outputs[0], outputs[1])
```

```python
import functools
import jax
import jax.numpy as jnp
from jax import lax
from jax.experimental import pallas as pl
from jax.experimental.pallas import tpu as pltpu
from jax.sharding import PartitionSpec as P

MESH = pl.DeviceIdType.MESH
PAD = 8


def halves(x):
    high = x.astype(jnp.bfloat16).astype(jnp.float32)
    return high, x - high


def product(left, right, turned):
    dims = (((1,), (1 if turned else 0,)), ((), ()))
    lh, ll = (h.astype(jnp.bfloat16) for h in halves(left))
    rh, rl = (h.astype(jnp.bfloat16) for h in halves(right))
    rows = jnp.concatenate([lh, ll], axis=1)
    if turned:
        other = jnp.concatenate([rh, rl], axis=0)
        other = jnp.concatenate([other, other], axis=1)
    else:
        other = jnp.concatenate([rh, rl], axis=1)
        other = jnp.concatenate([other, other], axis=0)
    out = lax.dot_general(rows, other, dims, preferred_element_type=jnp.float32)
    width = out.shape[1] // 2
    return out[:, :width] + out[:, width:]


def apply(rows, right, turned):
    count = rows.shape[0]
    dims = (((1,), (1 if turned else 0,)), ((), ()))
    stacked = jnp.concatenate(halves(rows), axis=0).astype(jnp.bfloat16)
    rh, rl = (h.astype(jnp.bfloat16) for h in halves(right))
    other = jnp.concatenate([rh, rl], axis=0 if turned else 1)
    out = lax.dot_general(stacked, other, dims, preferred_element_type=jnp.float32)
    width = out.shape[1] // 2
    out = out[:, :width] + out[:, width:]
    return out[:count] + out[count:]


def kernel(
    segs,
    blocks,
    rounds,
    jac_hbm,
    inv_hbm,
    inp_hbm,
    ctl_ref,
    step_ref,
    traj_ref,
    term_ref,
    gap_ref,
    count_ref,
    upd_ref,
    def_ref,
    jac,
    inv,
    inp,
    first,
    acc,
    got,
    enter,
    maps,
    full,
    vec_in,
    vec_out,
    load_sem,
    first_sem,
    map_send,
    map_recv,
    vec_send,
    vec_recv,
):
    slots, n = traj_ref.shape
    seg = lax.axis_index("seg")
    me = lax.axis_index("block")
    place = seg * blocks + me
    last = segs * blocks - 1
    lead = me == blocks - 1
    passes_on = jnp.logical_and(lead, seg + 1 < segs)

    loads = [
        pltpu.make_async_copy(src, dst, load_sem.at[i])
        for i, (src, dst) in enumerate(((jac_hbm, jac), (inv_hbm, inv), (inp_hbm, inp)))
    ]
    for load in loads:
        load.start()

    barrier = pltpu.get_barrier_semaphore()

    def tell(s, b):
        pl.semaphore_signal(barrier, inc=1, device_id=(s, b), device_id_type=MESH)

    @pl.when(place < last)
    def _():
        tell((place + 1) // blocks, (place + 1) % blocks)

    peers = jnp.where(place > 0, 1, 0)
    for r in range(rounds):
        half = 1 << r

        @pl.when((me // half) % 2 == 1)
        def _():
            tell(seg, (me // half) * half - 1)

        peers += jnp.where(
            me % (2 * half) == half - 1, jnp.minimum(half, blocks - 1 - me), 0
        )

    @pl.when(seg > 0)
    def _():
        tell(seg - 1, blocks - 1)

    peers += jnp.where(passes_on, blocks, 0)

    @pl.when(peers > 0)
    def _():
        pl.semaphore_wait(barrier, peers)

    ahead = jnp.maximum(place - 1, 0)
    first_copy = pltpu.make_async_remote_copy(
        src_ref=traj_ref.at[pl.ds(0, 1)],
        dst_ref=first,
        send_sem=first_sem.at[0],
        recv_sem=first_sem.at[1],
        device_id=(ahead // blocks, ahead % blocks),
        device_id_type=MESH,
    )

    @pl.when(place > 0)
    def _():
        first_copy.start()

    row = lax.broadcasted_iota(jnp.int32, (n, n), 0)
    col = lax.broadcasted_iota(jnp.int32, (n, n), 1)
    eye = jnp.where(row == col, 1.0, 0.0).astype(jnp.float32)
    live = [k < count_ref[0] for k in range(slots)]

    for load in loads:
        load.wait()

    trans = [
        eye + jnp.where(live[k], product(inv[k], jac[k], False), 0.0) for k in range(slots)
    ]
    running = [trans[0].T]
    for k in range(1, slots):
        running.append(product(running[-1], trans[k], True))
    for k in range(slots):
        maps[k, :n] = running[k]

    @pl.when(place < last)
    def _():
        first_copy.wait_recv()

    @pl.when(place == last)
    def _():
        first[...] = term_ref[...]

    upcoming = first[...]

    def eight(x):
        return jnp.broadcast_to(x, (PAD, x.shape[1]))

    nexts, offsets = [], []
    for k in range(slots):
        now = traj_ref[k : k + 1]
        if k + 1 < slots:
            nxt = jnp.where(live[k + 1], traj_ref[k + 1 : k + 2], upcoming)
        else:
            nxt = upcoming
        nexts.append(nxt)
        gap = eight(nxt - now)
        both = jnp.concatenate(
            [ctl_ref[k : k + 1], step_ref[k : k + 1], jnp.zeros((PAD - 2, ctl_ref.shape[1]), jnp.float32)],
            axis=0,
        )
        moved = apply(both, inp[k], True)
        mid = apply(gap, jac[k], True) * (1.0 / 12.0) - eight(0.5 * (nxt + now))
        defect = gap + apply(mid, jac[k], True) - eight(moved[0:1])
        def_ref[k : k + 1] = jnp.where(live[k], defect[0:1], 0.0)
        offset = apply(eight(moved[1:2]) - defect, inv[k], True)
        offsets.append(jnp.where(live[k], offset, 0.0))

    total = offsets[0]
    maps[0, n:] = total
    for k in range(1, slots):
        total = apply(total, trans[k], True) + offsets[k]
        maps[k, n:] = total
    acc[...] = maps[slots - 1]

    def compose(early, late):
        zeros = jnp.zeros((PAD, n), jnp.float32)
        rows = product(jnp.concatenate([early, zeros], axis=0), late[:n], False)
        tail = rows[n : n + PAD] + late[n:]
        return jnp.concatenate([rows[:n], tail], axis=0)

    def map_copy(r, to, j):
        return pltpu.make_async_remote_copy(
            src_ref=acc,
            dst_ref=got.at[r],
            send_sem=map_send.at[j],
            recv_sem=map_recv.at[r],
            device_id=(seg, to),
            device_id_type=MESH,
        )

    for r in range(rounds):
        half = 1 << r

        @pl.when(me % (2 * half) == half - 1)
        def _():
            for j in range(half, 0, -1):

                @pl.when(me + j < blocks)
                def _():
                    map_copy(r, me + j, j - 1).start()

        needed = jnp.logical_or(me % (2 * half) == 2 * half - 1, lead)

        @pl.when(jnp.logical_and(needed, (me // half) % 2 == 1))
        def _():
            map_copy(r, me, 0).wait_recv()
            acc[...] = compose(got[r], acc[...])

    def vec_copy(to):
        return pltpu.make_async_remote_copy(
            src_ref=vec_out,
            dst_ref=vec_in,
            send_sem=vec_send.at[to],
            recv_sem=vec_recv,
            device_id=(jnp.minimum(seg + 1, segs - 1), to),
            device_id_type=MESH,
        )

    @pl.when(seg == 0)
    def _():
        vec_in[...] = eight(gap_ref[...])

    @pl.when(passes_on)
    def _():
        @pl.when(seg > 0)
        def _():
            vec_copy(0).wait_recv()

        vec_out[...] = apply(vec_in[...], acc[:n], False) + acc[n:]
        for j in range(blocks - 1, -1, -1):
            vec_copy(j).start()

    enter[:n] = eye
    enter[n:] = jnp.zeros((PAD, n), jnp.float32)
    for r in reversed(range(rounds)):
        half = 1 << r
        bit = (me // half) % 2 == 1
        needed = jnp.logical_or(me % (2 * half) == 2 * half - 1, lead)

        @pl.when(jnp.logical_and(bit, jnp.logical_not(needed)))
        def _():
            map_copy(r, me, 0).wait_recv()

        @pl.when(bit)
        def _():
            enter[...] = compose(enter[...], got[r])

    start = enter[...]
    for k in range(slots):
        full[k] = compose(start, maps[k])

    @pl.when(jnp.logical_and(seg > 0, jnp.logical_not(passes_on)))
    def _():
        vec_copy(0).wait_recv()

    vec = vec_in[...]
    for k in range(slots):
        after = apply(vec, full[k, :n], False) + full[k, n:]
        upd_ref[k : k + 1] = jnp.where(live[k], nexts[k] + after[0:1], 0.0)

    @pl.when(place > 0)
    def _():
        first_copy.wait_send()

    for r in range(rounds):
        half = 1 << r

        @pl.when(me % (2 * half) == half - 1)
        def _():
            for j in range(half, 0, -1):

                @pl.when(me + j < blocks)
                def _():
                    map_copy(r, me + j, j - 1).wait_send()

    @pl.when(passes_on)
    def _():
        for j in range(blocks - 1, -1, -1):
            vec_copy(j).wait_send()


def body(
    jacobian,
    implicit_inv,
    input_map,
    controls,
    control_step,
    state_traj,
    terminal,
    init_gap,
    counts,
):
    segs, blocks = lax.axis_size("seg"), lax.axis_size("block")
    slots, n = state_traj.shape
    rounds = max(blocks - 1, 0).bit_length()
    anywhere = pl.BlockSpec(memory_space=pl.ANY)
    vmem = pl.BlockSpec(memory_space=pltpu.VMEM)
    smem = pl.BlockSpec(memory_space=pltpu.SMEM)
    f32 = jnp.float32
    shape = jax.ShapeDtypeStruct((slots, n), f32)
    return pl.pallas_call(
        functools.partial(kernel, segs, blocks, rounds),
        out_shape=(shape, shape),
        in_specs=[anywhere] * 3 + [vmem] * 5 + [smem],
        out_specs=(vmem, vmem),
        scratch_shapes=[
            pltpu.VMEM(jacobian.shape, f32),
            pltpu.VMEM(implicit_inv.shape, f32),
            pltpu.VMEM(input_map.shape, f32),
            pltpu.VMEM((1, n), f32),
            pltpu.VMEM((n + PAD, n), f32),
            pltpu.VMEM((max(rounds, 1), n + PAD, n), f32),
            pltpu.VMEM((n + PAD, n), f32),
            pltpu.VMEM((slots, n + PAD, n), f32),
            pltpu.VMEM((slots, n + PAD, n), f32),
            pltpu.VMEM((PAD, n), f32),
            pltpu.VMEM((PAD, n), f32),
            pltpu.SemaphoreType.DMA((3,)),
            pltpu.SemaphoreType.DMA((2,)),
            pltpu.SemaphoreType.DMA((blocks,)),
            pltpu.SemaphoreType.DMA((max(rounds, 1),)),
            pltpu.SemaphoreType.DMA((blocks,)),
            pltpu.SemaphoreType.DMA,
        ],
        compiler_params=pltpu.CompilerParams(
            collective_id=0, has_side_effects=True, vmem_limit_bytes=24 * 1024 * 1024
        ),
    )(
        jacobian,
        implicit_inv,
        input_map,
        controls,
        control_step,
        state_traj,
        terminal[None],
        init_gap[None],
        counts,
    )


def solution(mesh):
    in_specs = (
        P(("seg", "block"), None, None),
        P(("seg", "block"), None, None),
        P(("seg", "block"), None, None),
        P(("seg", "block"), None),
        P(("seg", "block"), None),
        P(("seg", "block"), None),
        P(),
        P(),
        P(("seg", "block")),
    )
    out_specs = (P(("seg", "block"), None), P(("seg", "block"), None))
    return jax.shard_map(body, mesh=mesh, in_specs=in_specs, out_specs=out_specs, check_vma=False)
```

```python
import functools
import jax
import jax.numpy as jnp
from jax import lax
from jax.experimental import pallas as pl
from jax.experimental.pallas import tpu as pltpu
from jax.sharding import PartitionSpec as P

MESH = pl.DeviceIdType.MESH
PAD = 8


def halves(x):
    high = x.astype(jnp.bfloat16).astype(jnp.float32)
    return high, x - high


def product(left, right, turned):
    dims = (((1,), (1 if turned else 0,)), ((), ()))
    lh, ll = (h.astype(jnp.bfloat16) for h in halves(left))
    rh, rl = (h.astype(jnp.bfloat16) for h in halves(right))
    rows = jnp.concatenate([lh, ll], axis=1)
    if turned:
        other = jnp.concatenate([rh, rl], axis=0)
        other = jnp.concatenate([other, other], axis=1)
    else:
        other = jnp.concatenate([rh, rl], axis=1)
        other = jnp.concatenate([other, other], axis=0)
    out = lax.dot_general(rows, other, dims, preferred_element_type=jnp.float32)
    width = out.shape[1] // 2
    return out[:, :width] + out[:, width:]


def apply(rows, right, turned):
    count = rows.shape[0]
    dims = (((1,), (1 if turned else 0,)), ((), ()))
    stacked = jnp.concatenate(halves(rows), axis=0).astype(jnp.bfloat16)
    rh, rl = (h.astype(jnp.bfloat16) for h in halves(right))
    other = jnp.concatenate([rh, rl], axis=0 if turned else 1)
    out = lax.dot_general(stacked, other, dims, preferred_element_type=jnp.float32)
    width = out.shape[1] // 2
    out = out[:, :width] + out[:, width:]
    return out[:count] + out[count:]


def compose(early, late):
    n = late.shape[1]
    zeros = jnp.zeros((PAD, n), jnp.float32)
    rows = product(jnp.concatenate([early, zeros], axis=0), late[:n], False)
    tail = rows[n : n + PAD] + late[n:]
    return jnp.concatenate([rows[:n], tail], axis=0)


def kernel(
    segs,
    blocks,
    rounds,
    jac_hbm,
    inv_hbm,
    inp_hbm,
    ctl_hbm,
    step_hbm,
    traj_hbm,
    term_hbm,
    gap_hbm,
    count_hbm,
    out_ref,
    jac,
    inv,
    inp,
    ctl,
    step,
    traj,
    term,
    gap,
    count,
    first,
    acc,
    got,
    enter,
    maps,
    full,
    vec_in,
    vec_out,
    load_sem,
    first_sem,
    map_send,
    map_recv,
    vec_send,
    vec_recv,
):
    slots, n = traj.shape
    seg = lax.axis_index("seg")
    me = lax.axis_index("block")
    place = seg * blocks + me
    last = segs * blocks - 1
    odd = me % 2 == 1
    even = me % 2 == 0
    mate = me + 1 - 2 * (me % 2)
    passes_on = jnp.logical_and(odd, seg + 1 < segs)

    loads = [
        pltpu.make_async_copy(src, dst, load_sem.at[i])
        for i, (src, dst) in enumerate(
            (
                (traj_hbm, traj),
                (count_hbm, count),
                (jac_hbm, jac),
                (inv_hbm, inv),
                (inp_hbm, inp),
                (ctl_hbm, ctl),
                (step_hbm, step),
                (term_hbm, term),
                (gap_hbm, gap),
            )
        )
    ]
    for load in loads:
        load.start()

    barrier = pltpu.get_barrier_semaphore()

    def tell(s, b):
        pl.semaphore_signal(barrier, inc=1, device_id=(s, b), device_id_type=MESH)

    def partner(r):
        half = 1 << r
        return me + half - 2 * half * ((me // half) % 2)

    tell(seg, mate)

    @pl.when(place < last)
    def _():
        tell((place + 1) // blocks, (place + 1) % blocks)

    @pl.when(odd)
    def _():
        for r in range(1, rounds):
            tell(seg, partner(r))

    @pl.when(seg > 0)
    def _():
        tell(seg - 1, me + 1 - me % 2)

    peers = 1 + jnp.where(place > 0, 1, 0) + jnp.where(odd, rounds - 1, 0)
    peers += jnp.where(passes_on, 2, 0)
    pl.semaphore_wait(barrier, peers)

    ahead = jnp.maximum(place - 1, 0)
    first_copy = pltpu.make_async_remote_copy(
        src_ref=traj.at[pl.ds(0, 1)],
        dst_ref=first,
        send_sem=first_sem.at[0],
        recv_sem=first_sem.at[1],
        device_id=(ahead // blocks, ahead % blocks),
        device_id_type=MESH,
    )
    loads[0].wait()

    @pl.when(place > 0)
    def _():
        first_copy.start()

    row = lax.broadcasted_iota(jnp.int32, (n, n), 0)
    col = lax.broadcasted_iota(jnp.int32, (n, n), 1)
    eye = jnp.where(row == col, 1.0, 0.0).astype(jnp.float32)
    for load in loads[1:]:
        load.wait()
    live = [k < count[0] for k in range(slots)]

    trans = [
        eye + jnp.where(live[k], product(inv[k], jac[k], False), 0.0) for k in range(slots)
    ]
    known = {}

    def fold(lo, hi):
        if (lo, hi) not in known:
            if hi - lo == 1:
                known[lo, hi] = trans[lo].T
            else:
                mid = (lo + hi) // 2 if lo or hi == slots else hi - 1
                early = fold(lo, mid)
                if hi - mid == 1:
                    known[lo, hi] = product(early, trans[mid], True)
                else:
                    known[lo, hi] = product(early, fold(mid, hi), False)
        return known[lo, hi]

    acc[0, :n] = fold(0, slots)

    @pl.when(place < last)
    def _():
        first_copy.wait_recv()

    @pl.when(place == last)
    def _():
        first[...] = term[...]

    upcoming = first[...]

    def eight(x):
        return jnp.broadcast_to(x, (PAD, x.shape[1]))

    nexts, offsets = [], []
    for k in range(slots):
        now = traj[k : k + 1]
        if k + 1 < slots:
            nxt = jnp.where(live[k + 1], traj[k + 1 : k + 2], upcoming)
        else:
            nxt = upcoming
        nexts.append(nxt)
        change = eight(nxt - now)
        both = jnp.concatenate(
            [ctl[k : k + 1], step[k : k + 1], jnp.zeros((PAD - 2, ctl.shape[1]), jnp.float32)],
            axis=0,
        )
        moved = apply(both, inp[k], False)
        mid = apply(change, jac[k], True) * (1.0 / 12.0) - eight(0.5 * (nxt + now))
        defect = change + apply(mid, jac[k], True) - eight(moved[0:1])
        out_ref[1, k : k + 1] = jnp.where(live[k], defect[0:1], 0.0)
        offset = apply(eight(moved[1:2]) - defect, inv[k], True)
        offsets.append(jnp.where(live[k], offset, 0.0))
    known_vec = {}

    def fold_vec(lo, hi):
        if (lo, hi) not in known_vec:
            if hi - lo == 1:
                known_vec[lo, hi] = offsets[lo]
            else:
                mid = (lo + hi) // 2 if lo or hi == slots else hi - 1
                early = fold_vec(lo, mid)
                if hi - mid == 1:
                    moved = apply(early, trans[mid], True)
                else:
                    moved = apply(early, fold(mid, hi), False)
                known_vec[lo, hi] = moved + fold_vec(mid, hi)
        return known_vec[lo, hi]

    acc[0, n:] = fold_vec(0, slots)

    def map_copy(src, r, to):
        return pltpu.make_async_remote_copy(
            src_ref=src,
            dst_ref=got.at[r],
            send_sem=map_send.at[r],
            recv_sem=map_recv.at[r],
            device_id=(seg, to),
            device_id_type=MESH,
        )

    @pl.when(even)
    def _():
        map_copy(acc.at[0], 0, mate).start()

    for k in range(slots):
        maps[k, :n] = fold(0, k + 1)
        maps[k, n:] = fold_vec(0, k + 1)

    @pl.when(odd)
    def _():
        map_copy(acc.at[0], 0, mate).wait_recv()
        acc[1] = compose(got[0], acc[0])
        for r in range(1, rounds):
            map_copy(acc.at[r], r, partner(r)).start()
            if r == 1:
                enter[:n] = eye
                enter[n:] = jnp.zeros((PAD, n), jnp.float32)
            map_copy(acc.at[r], r, partner(r)).wait_recv()
            high = (me // (1 << r)) % 2 == 1

            @pl.when(high)
            def _():
                acc[r + 1] = compose(got[r], acc[r])
                enter[...] = compose(got[r], enter[...])

            @pl.when(jnp.logical_not(high))
            def _():
                acc[r + 1] = compose(acc[r], got[r])

        map_copy(enter, rounds, mate).start()

    def vec_copy(i):
        return pltpu.make_async_remote_copy(
            src_ref=vec_out,
            dst_ref=vec_in,
            send_sem=vec_send.at[i],
            recv_sem=vec_recv,
            device_id=(jnp.minimum(seg + 1, segs - 1), me + 1 - me % 2 - i),
            device_id_type=MESH,
        )

    @pl.when(seg == 0)
    def _():
        vec_in[...] = eight(gap[...])

    @pl.when(passes_on)
    def _():
        @pl.when(seg > 0)
        def _():
            vec_copy(0).wait_recv()

        vec_out[...] = apply(vec_in[...], acc[rounds, :n], False) + acc[rounds, n:]
        for i in range(2):
            vec_copy(i).start()

    @pl.when(even)
    def _():
        map_copy(enter, rounds, mate).wait_recv()
        start = got[rounds]
        for k in range(slots):
            full[k] = compose(start, maps[k])

    @pl.when(odd)
    def _():
        start = compose(enter[...], got[0])
        for k in range(slots):
            full[k] = compose(start, maps[k])

    @pl.when(jnp.logical_and(seg > 0, jnp.logical_not(passes_on)))
    def _():
        vec_copy(0).wait_recv()

    vec = vec_in[...]
    for k in range(slots):
        after = apply(vec, full[k, :n], False) + full[k, n:]
        out_ref[0, k : k + 1] = jnp.where(live[k], nexts[k] + after[0:1], 0.0)

    @pl.when(place > 0)
    def _():
        first_copy.wait_send()

    @pl.when(even)
    def _():
        map_copy(acc.at[0], 0, mate).wait_send()

    @pl.when(odd)
    def _():
        for r in range(1, rounds):
            map_copy(acc.at[r], r, partner(r)).wait_send()
        map_copy(enter, rounds, mate).wait_send()

    @pl.when(passes_on)
    def _():
        for i in range(2):
            vec_copy(i).wait_send()


def body(
    jacobian,
    implicit_inv,
    input_map,
    controls,
    control_step,
    state_traj,
    terminal,
    init_gap,
    counts,
):
    segs, blocks = lax.axis_size("seg"), lax.axis_size("block")
    slots, n = state_traj.shape
    rounds = blocks.bit_length() - 1
    if blocks < 4 or blocks != 1 << rounds:
        raise ValueError("blocks")
    f32 = jnp.float32
    operands = (
        jacobian,
        implicit_inv,
        jnp.swapaxes(input_map, 1, 2),
        controls,
        control_step,
        state_traj,
        terminal[None],
        init_gap[None],
        counts,
    )
    out = pl.pallas_call(
        functools.partial(kernel, segs, blocks, rounds),
        out_shape=jax.ShapeDtypeStruct((2, slots, n), f32),
        in_specs=[pl.BlockSpec(memory_space=pltpu.HBM)] * len(operands),
        out_specs=pl.BlockSpec(memory_space=pltpu.VMEM),
        scratch_shapes=[pltpu.VMEM(x.shape, f32) for x in operands[:-1]]
        + [
            pltpu.SMEM(counts.shape, jnp.int32),
            pltpu.VMEM((1, n), f32),
            pltpu.VMEM((rounds + 1, n + PAD, n), f32),
            pltpu.VMEM((rounds + 1, n + PAD, n), f32),
            pltpu.VMEM((n + PAD, n), f32),
            pltpu.VMEM((slots, n + PAD, n), f32),
            pltpu.VMEM((slots, n + PAD, n), f32),
            pltpu.VMEM((PAD, n), f32),
            pltpu.VMEM((PAD, n), f32),
            pltpu.SemaphoreType.DMA((len(operands),)),
            pltpu.SemaphoreType.DMA((2,)),
            pltpu.SemaphoreType.DMA((rounds + 1,)),
            pltpu.SemaphoreType.DMA((rounds + 1,)),
            pltpu.SemaphoreType.DMA((2,)),
            pltpu.SemaphoreType.DMA,
        ],
        compiler_params=pltpu.CompilerParams(
            collective_id=0, has_side_effects=True, vmem_limit_bytes=60 * 1024 * 1024
        ),
    )(*operands)
    return out[0], out[1]


def solution(mesh):
    in_specs = (
        P(("seg", "block"), None, None),
        P(("seg", "block"), None, None),
        P(("seg", "block"), None, None),
        P(("seg", "block"), None),
        P(("seg", "block"), None),
        P(("seg", "block"), None),
        P(),
        P(),
        P(("seg", "block")),
    )
    out_specs = (P(("seg", "block"), None), P(("seg", "block"), None))
    return jax.shard_map(body, mesh=mesh, in_specs=in_specs, out_specs=out_specs, check_vma=False)
```

```python
import functools
import jax
import jax.numpy as jnp
from jax import lax
from jax.experimental import pallas as pl
from jax.experimental.pallas import tpu as pltpu
from jax.sharding import PartitionSpec as P

MESH = pl.DeviceIdType.MESH
PAD = 8


def halves(x):
    high = x.astype(jnp.bfloat16).astype(jnp.float32)
    return high, x - high


def product(left, right, turned):
    dims = (((1,), (1 if turned else 0,)), ((), ()))
    lh, ll = (h.astype(jnp.bfloat16) for h in halves(left))
    rh, rl = (h.astype(jnp.bfloat16) for h in halves(right))
    rows = jnp.concatenate([lh, ll], axis=1)
    if turned:
        other = jnp.concatenate([rh, rl], axis=0)
        other = jnp.concatenate([other, other], axis=1)
    else:
        other = jnp.concatenate([rh, rl], axis=1)
        other = jnp.concatenate([other, other], axis=0)
    out = lax.dot_general(rows, other, dims, preferred_element_type=jnp.float32)
    width = out.shape[1] // 2
    return out[:, :width] + out[:, width:]


def apply(rows, right, turned):
    count = rows.shape[0]
    dims = (((1,), (1 if turned else 0,)), ((), ()))
    stacked = jnp.concatenate(halves(rows), axis=0).astype(jnp.bfloat16)
    rh, rl = (h.astype(jnp.bfloat16) for h in halves(right))
    other = jnp.concatenate([rh, rl], axis=0 if turned else 1)
    out = lax.dot_general(stacked, other, dims, preferred_element_type=jnp.float32)
    width = out.shape[1] // 2
    out = out[:, :width] + out[:, width:]
    return out[:count] + out[count:]


def compose(early, late):
    n = late.shape[1]
    zeros = jnp.zeros((PAD, n), jnp.float32)
    rows = product(jnp.concatenate([early, zeros], axis=0), late[:n], False)
    tail = rows[n : n + PAD] + late[n:]
    return jnp.concatenate([rows[:n], tail], axis=0)


def kernel(
    segs,
    blocks,
    rounds,
    jac_hbm,
    inv_hbm,
    inp_hbm,
    ctl_hbm,
    step_hbm,
    traj_hbm,
    term_hbm,
    gap_hbm,
    count_hbm,
    out_ref,
    jac,
    inv,
    inp,
    ctl,
    step,
    traj,
    term,
    gap,
    count,
    first,
    acc,
    got,
    enter,
    maps,
    full,
    tails,
    vec_in,
    vec_out,
    load_sem,
    first_sem,
    map_send,
    map_recv,
    vec_send,
    vec_recv,
):
    slots, n = traj.shape
    seg = lax.axis_index("seg")
    me = lax.axis_index("block")
    place = seg * blocks + me
    last = segs * blocks - 1
    passes_on = jnp.logical_and(me == blocks - 1, seg + 1 < segs)

    loads = [
        pltpu.make_async_copy(src, dst, load_sem.at[i])
        for i, (src, dst) in enumerate(
            (
                (traj_hbm, traj),
                (count_hbm, count),
                (jac_hbm, jac),
                (inv_hbm, inv),
                (inp_hbm, inp),
                (ctl_hbm, ctl),
                (step_hbm, step),
                (term_hbm, term),
                (gap_hbm, gap),
            )
        )
    ]
    for load in loads:
        load.start()

    barrier = pltpu.get_barrier_semaphore()

    def tell(s, b):
        pl.semaphore_signal(barrier, inc=1, device_id=(s, b), device_id_type=MESH)

    @pl.when(place < last)
    def _():
        tell((place + 1) // blocks, (place + 1) % blocks)

    peers = jnp.where(place > 0, 1, 0)
    for r in range(rounds):
        half = 1 << r

        @pl.when((me // half) % 2 == 1)
        def _():
            tell(seg, (me // half) * half - 1)

        peers += jnp.where(me % (2 * half) == half - 1, half, 0)

    @pl.when(seg > 0)
    def _():
        tell(seg - 1, blocks - 1)

    peers += jnp.where(passes_on, blocks, 0)
    pl.semaphore_wait(barrier, peers)

    ahead = jnp.maximum(place - 1, 0)
    first_copy = pltpu.make_async_remote_copy(
        src_ref=traj.at[pl.ds(0, 1)],
        dst_ref=first,
        send_sem=first_sem.at[0],
        recv_sem=first_sem.at[1],
        device_id=(ahead // blocks, ahead % blocks),
        device_id_type=MESH,
    )
    loads[0].wait()

    @pl.when(place > 0)
    def _():
        first_copy.start()

    row = lax.broadcasted_iota(jnp.int32, (n, n), 0)
    col = lax.broadcasted_iota(jnp.int32, (n, n), 1)
    eye = jnp.where(row == col, 1.0, 0.0).astype(jnp.float32)
    for load in loads[1:]:
        load.wait()
    live = [k < count[0] for k in range(slots)]

    @pl.when(place < last)
    def _():
        first_copy.wait_recv()

    @pl.when(place == last)
    def _():
        first[...] = term[...]

    trans = [
        eye + jnp.where(live[k], product(inv[k], jac[k], False), 0.0) for k in range(slots)
    ]
    known = {}

    def fold(lo, hi):
        if (lo, hi) not in known:
            if hi - lo == 1:
                known[lo, hi] = trans[lo].T
            else:
                mid = (lo + hi) // 2 if lo or hi == slots else hi - 1
                early = fold(lo, mid)
                if hi - mid == 1:
                    known[lo, hi] = product(early, trans[mid], True)
                else:
                    known[lo, hi] = product(early, fold(mid, hi), False)
        return known[lo, hi]

    acc[:n] = fold(0, slots)

    upcoming = first[...]

    def eight(x):
        return jnp.broadcast_to(x, (PAD, x.shape[1]))

    nexts, offsets = [], []
    for k in range(slots):
        now = traj[k : k + 1]
        if k + 1 < slots:
            nxt = jnp.where(live[k + 1], traj[k + 1 : k + 2], upcoming)
        else:
            nxt = upcoming
        nexts.append(nxt)
        change = eight(nxt - now)
        both = jnp.concatenate(
            [ctl[k : k + 1], step[k : k + 1], jnp.zeros((PAD - 2, ctl.shape[1]), jnp.float32)],
            axis=0,
        )
        moved = apply(both, inp[k], False)
        mid = apply(change, jac[k], True) * (1.0 / 12.0) - eight(0.5 * (nxt + now))
        defect = change + apply(mid, jac[k], True) - eight(moved[0:1])
        out_ref[1, k : k + 1] = jnp.where(live[k], defect[0:1], 0.0)
        offset = apply(eight(moved[1:2]) - defect, inv[k], True)
        offsets.append(jnp.where(live[k], offset, 0.0))
    known_vec = {}

    def fold_vec(lo, hi):
        if (lo, hi) not in known_vec:
            if hi - lo == 1:
                known_vec[lo, hi] = offsets[lo]
            else:
                mid = (lo + hi) // 2 if lo or hi == slots else hi - 1
                early = fold_vec(lo, mid)
                if hi - mid == 1:
                    moved = apply(early, trans[mid], True)
                else:
                    moved = apply(early, fold(mid, hi), False)
                known_vec[lo, hi] = moved + fold_vec(mid, hi)
        return known_vec[lo, hi]

    acc[n:] = fold_vec(0, slots)

    def map_copy(r, to, j):
        return pltpu.make_async_remote_copy(
            src_ref=acc,
            dst_ref=got.at[r],
            send_sem=map_send.at[j],
            recv_sem=map_recv.at[r],
            device_id=(seg, to),
            device_id_type=MESH,
        )

    for r in range(rounds):
        half = 1 << r

        @pl.when(me % (2 * half) == half - 1)
        def _():
            for j in range(half, 0, -1):
                map_copy(r, me + j, j - 1).start()

        @pl.when(jnp.logical_and(me % (2 * half) == 2 * half - 1, me < blocks - 1))
        def _():
            map_copy(r, me, 0).wait_recv()
            acc[...] = compose(got[r], acc[...])

    for k in range(slots):
        maps[k, :n] = fold(0, k + 1)
        maps[k, n:] = fold_vec(0, k + 1)

    enter[:n] = eye
    enter[n:] = jnp.zeros((PAD, n), jnp.float32)
    for r in reversed(range(rounds)):
        half = 1 << r
        done = jnp.logical_and(me % (2 * half) == 2 * half - 1, me < blocks - 1)

        @pl.when((me // half) % 2 == 1)
        def _():
            @pl.when(jnp.logical_not(done))
            def _():
                map_copy(r, me, 0).wait_recv()

            enter[...] = compose(enter[...], got[r])

    start = enter[...]
    for k in reversed(range(slots)):
        rows = compose(start, maps[k])
        full[k] = jnp.concatenate(halves(rows[:n]), axis=1).astype(jnp.bfloat16)
        tails[k] = rows[n:]

    def vec_copy(to):
        return pltpu.make_async_remote_copy(
            src_ref=vec_out,
            dst_ref=vec_in,
            send_sem=vec_send.at[to],
            recv_sem=vec_recv,
            device_id=(jnp.minimum(seg + 1, segs - 1), to),
            device_id_type=MESH,
        )

    @pl.when(seg == 0)
    def _():
        vec_in[...] = eight(gap[...])

    @pl.when(seg > 0)
    def _():
        vec_copy(0).wait_recv()

    stacked = jnp.concatenate(halves(vec_in[...]), axis=0).astype(jnp.bfloat16)

    def after(k):
        rows = jnp.dot(stacked, full[k], preferred_element_type=jnp.float32)
        rows = rows[:, :n] + rows[:, n:]
        return rows[:PAD] + rows[PAD:] + tails[k]

    @pl.when(passes_on)
    def _():
        vec_out[...] = after(slots - 1)
        for to in range(blocks - 1, -1, -1):
            vec_copy(to).start()

    for k in range(slots):
        out_ref[0, k : k + 1] = jnp.where(live[k], nexts[k] + after(k)[0:1], 0.0)

    @pl.when(place > 0)
    def _():
        first_copy.wait_send()

    for r in range(rounds):
        half = 1 << r

        @pl.when(me % (2 * half) == half - 1)
        def _():
            for j in range(half, 0, -1):
                map_copy(r, me + j, j - 1).wait_send()

    @pl.when(passes_on)
    def _():
        for to in range(blocks):
            vec_copy(to).wait_send()


def body(
    jacobian,
    implicit_inv,
    input_map,
    controls,
    control_step,
    state_traj,
    terminal,
    init_gap,
    counts,
):
    segs, blocks = lax.axis_size("seg"), lax.axis_size("block")
    slots, n = state_traj.shape
    rounds = blocks.bit_length() - 1
    if blocks < 4 or blocks != 1 << rounds:
        raise ValueError("blocks")
    f32 = jnp.float32
    operands = (
        jacobian,
        implicit_inv,
        jnp.swapaxes(input_map, 1, 2),
        controls,
        control_step,
        state_traj,
        terminal[None],
        init_gap[None],
        counts,
    )
    out = pl.pallas_call(
        functools.partial(kernel, segs, blocks, rounds),
        out_shape=jax.ShapeDtypeStruct((2, slots, n), f32),
        in_specs=[pl.BlockSpec(memory_space=pltpu.HBM)] * len(operands),
        out_specs=pl.BlockSpec(memory_space=pltpu.VMEM),
        scratch_shapes=[pltpu.VMEM(x.shape, f32) for x in operands[:-1]]
        + [
            pltpu.SMEM(counts.shape, jnp.int32),
            pltpu.VMEM((1, n), f32),
            pltpu.VMEM((n + PAD, n), f32),
            pltpu.VMEM((rounds, n + PAD, n), f32),
            pltpu.VMEM((n + PAD, n), f32),
            pltpu.VMEM((slots, n + PAD, n), f32),
            pltpu.VMEM((slots, n, 2 * n), jnp.bfloat16),
            pltpu.VMEM((slots, PAD, n), f32),
            pltpu.VMEM((PAD, n), f32),
            pltpu.VMEM((PAD, n), f32),
            pltpu.SemaphoreType.DMA((len(operands),)),
            pltpu.SemaphoreType.DMA((2,)),
            pltpu.SemaphoreType.DMA((blocks,)),
            pltpu.SemaphoreType.DMA((rounds,)),
            pltpu.SemaphoreType.DMA((blocks,)),
            pltpu.SemaphoreType.DMA,
        ],
        compiler_params=pltpu.CompilerParams(
            collective_id=0, has_side_effects=True, vmem_limit_bytes=60 * 1024 * 1024
        ),
    )(*operands)
    return out[0], out[1]


def solution(mesh):
    in_specs = (
        P(("seg", "block"), None, None),
        P(("seg", "block"), None, None),
        P(("seg", "block"), None, None),
        P(("seg", "block"), None),
        P(("seg", "block"), None),
        P(("seg", "block"), None),
        P(),
        P(),
        P(("seg", "block")),
    )
    out_specs = (P(("seg", "block"), None), P(("seg", "block"), None))
    return jax.shard_map(body, mesh=mesh, in_specs=in_specs, out_specs=out_specs, check_vma=False)
```

```python
import functools
import jax
import jax.numpy as jnp
from jax import lax
from jax.experimental import pallas as pl
from jax.experimental.pallas import tpu as pltpu
from jax.sharding import PartitionSpec as P

MESH = pl.DeviceIdType.MESH
PAD = 8


def halves(x):
    high = x.astype(jnp.bfloat16).astype(jnp.float32)
    return high, x - high


def product(left, right, turned):
    dims = (((1,), (1 if turned else 0,)), ((), ()))
    lh, ll = (h.astype(jnp.bfloat16) for h in halves(left))
    rh, rl = (h.astype(jnp.bfloat16) for h in halves(right))
    rows = jnp.concatenate([lh, ll], axis=1)
    if turned:
        other = jnp.concatenate([rh, rl], axis=0)
        other = jnp.concatenate([other, other], axis=1)
    else:
        other = jnp.concatenate([rh, rl], axis=1)
        other = jnp.concatenate([other, other], axis=0)
    out = lax.dot_general(rows, other, dims, preferred_element_type=jnp.float32)
    width = out.shape[1] // 2
    return out[:, :width] + out[:, width:]


def apply(rows, right, turned):
    count = rows.shape[0]
    dims = (((1,), (1 if turned else 0,)), ((), ()))
    stacked = jnp.concatenate(halves(rows), axis=0).astype(jnp.bfloat16)
    rh, rl = (h.astype(jnp.bfloat16) for h in halves(right))
    other = jnp.concatenate([rh, rl], axis=0 if turned else 1)
    out = lax.dot_general(stacked, other, dims, preferred_element_type=jnp.float32)
    width = out.shape[1] // 2
    out = out[:, :width] + out[:, width:]
    return out[:count] + out[count:]


def compose(early, late):
    n = late.shape[1]
    zeros = jnp.zeros((PAD, n), jnp.float32)
    rows = product(jnp.concatenate([early, zeros], axis=0), late[:n], False)
    tail = rows[n : n + PAD] + late[n:]
    return jnp.concatenate([rows[:n], tail], axis=0)


def kernel(
    segs,
    blocks,
    rounds,
    jac_hbm,
    inv_hbm,
    inp_hbm,
    ctl_hbm,
    step_hbm,
    traj_hbm,
    term_hbm,
    gap_hbm,
    count_hbm,
    out_ref,
    jac,
    inv,
    inp,
    ctl,
    step,
    traj,
    term,
    gap,
    count,
    first,
    acc,
    got,
    enter,
    maps,
    full,
    tails,
    vec_in,
    vec_out,
    load_sem,
    first_sem,
    map_send,
    map_recv,
    vec_send,
    vec_recv,
):
    slots, n = traj.shape
    seg = lax.axis_index("seg")
    me = lax.axis_index("block")
    place = seg * blocks + me
    last = segs * blocks - 1
    passes_on = jnp.logical_and(me == blocks - 1, seg + 1 < segs)

    loads = [
        pltpu.make_async_copy(src, dst, load_sem.at[i])
        for i, (src, dst) in enumerate(
            (
                (traj_hbm, traj),
                (count_hbm, count),
                (jac_hbm, jac),
                (inv_hbm, inv),
                (inp_hbm, inp),
                (ctl_hbm, ctl),
                (step_hbm, step),
                (term_hbm, term),
                (gap_hbm, gap),
            )
        )
    ]
    for load in loads:
        load.start()

    barrier = pltpu.get_barrier_semaphore()

    def tell(s, b):
        pl.semaphore_signal(barrier, inc=1, device_id=(s, b), device_id_type=MESH)

    @pl.when(place < last)
    def _():
        tell((place + 1) // blocks, (place + 1) % blocks)

    peers = jnp.where(place > 0, 1, 0)
    for r in range(rounds):
        half = 1 << r

        @pl.when((me // half) % 2 == 1)
        def _():
            tell(seg, (me // half) * half - 1)

        peers += jnp.where(me % (2 * half) == half - 1, half, 0)

    @pl.when(seg > 0)
    def _():
        tell(seg - 1, blocks - 1)

    peers += jnp.where(passes_on, blocks, 0)
    pl.semaphore_wait(barrier, peers)

    ahead = jnp.maximum(place - 1, 0)
    first_copy = pltpu.make_async_remote_copy(
        src_ref=traj.at[pl.ds(0, 1)],
        dst_ref=first,
        send_sem=first_sem.at[0],
        recv_sem=first_sem.at[1],
        device_id=(ahead // blocks, ahead % blocks),
        device_id_type=MESH,
    )
    loads[0].wait()

    @pl.when(place > 0)
    def _():
        first_copy.start()

    row = lax.broadcasted_iota(jnp.int32, (n, n), 0)
    col = lax.broadcasted_iota(jnp.int32, (n, n), 1)
    eye = jnp.where(row == col, 1.0, 0.0).astype(jnp.float32)
    for load in loads[1:]:
        load.wait()
    live = [k < count[0] for k in range(slots)]

    @pl.when(place < last)
    def _():
        first_copy.wait_recv()

    @pl.when(place == last)
    def _():
        first[...] = term[...]

    trans = [
        eye + jnp.where(live[k], product(inv[k], jac[k], False), 0.0) for k in range(slots)
    ]
    known = {}

    def fold(lo, hi):
        if (lo, hi) not in known:
            if hi - lo == 1:
                known[lo, hi] = trans[lo].T
            else:
                mid = (lo + hi) // 2 if lo or hi == slots else hi - 1
                early = fold(lo, mid)
                if hi - mid == 1:
                    known[lo, hi] = product(early, trans[mid], True)
                else:
                    known[lo, hi] = product(early, fold(mid, hi), False)
        return known[lo, hi]

    acc[:n] = fold(0, slots)

    upcoming = first[...]

    def eight(x):
        return jnp.broadcast_to(x, (PAD, x.shape[1]))

    nexts, offsets = [], []
    for k in range(slots):
        now = traj[k : k + 1]
        if k + 1 < slots:
            nxt = jnp.where(live[k + 1], traj[k + 1 : k + 2], upcoming)
        else:
            nxt = upcoming
        nexts.append(nxt)
        change = eight(nxt - now)
        both = jnp.concatenate(
            [ctl[k : k + 1], step[k : k + 1], jnp.zeros((PAD - 2, ctl.shape[1]), jnp.float32)],
            axis=0,
        )
        moved = apply(both, inp[k], False)
        mid = apply(change, jac[k], True) * (1.0 / 12.0) - eight(0.5 * (nxt + now))
        defect = change + apply(mid, jac[k], True) - eight(moved[0:1])
        out_ref[1, k : k + 1] = jnp.where(live[k], defect[0:1], 0.0)
        offset = apply(eight(moved[1:2]) - defect, inv[k], True)
        offsets.append(jnp.where(live[k], offset, 0.0))
    known_vec = {}

    def fold_vec(lo, hi):
        if (lo, hi) not in known_vec:
            if hi - lo == 1:
                known_vec[lo, hi] = offsets[lo]
            else:
                mid = (lo + hi) // 2 if lo or hi == slots else hi - 1
                early = fold_vec(lo, mid)
                if hi - mid == 1:
                    moved = apply(early, trans[mid], True)
                else:
                    moved = apply(early, fold(mid, hi), False)
                known_vec[lo, hi] = moved + fold_vec(mid, hi)
        return known_vec[lo, hi]

    acc[n:] = fold_vec(0, slots)

    def at_front(r):
        return jnp.logical_and(seg == 0, me < (2 << r))

    def gives(r):
        half = 1 << r
        return jnp.logical_and(me % (2 * half) == half - 1, jnp.logical_not(at_front(r)))

    def gathers(r):
        half = 1 << r
        inner = jnp.logical_and(me % (2 * half) == 2 * half - 1, me < blocks - 1)
        return jnp.logical_and(inner, jnp.logical_not(at_front(r)))

    def takes(r):
        return jnp.logical_and((me // (1 << r)) % 2 == 1, jnp.logical_not(at_front(r)))

    def map_copy(r, to, j):
        return pltpu.make_async_remote_copy(
            src_ref=acc,
            dst_ref=got.at[r],
            send_sem=map_send.at[j],
            recv_sem=map_recv.at[r],
            device_id=(seg, to),
            device_id_type=MESH,
        )

    for r in range(rounds):

        @pl.when(gives(r))
        def _():
            for j in range(1 << r, 0, -1):
                map_copy(r, me + j, j - 1).start()

        @pl.when(gathers(r))
        def _():
            map_copy(r, me, 0).wait_recv()
            acc[...] = compose(got[r], acc[...])

    for k in range(slots):
        maps[k, :n] = fold(0, k + 1)
        maps[k, n:] = fold_vec(0, k + 1)

    some = takes(0)
    for r in range(1, rounds):
        some = jnp.logical_or(some, takes(r))

    def keep(k, rows):
        full[k] = jnp.concatenate(halves(rows[:n]), axis=1).astype(jnp.bfloat16)
        tails[k] = rows[n:]

    @pl.when(jnp.logical_not(some))
    def _():
        for k in range(slots):
            keep(k, maps[k])

    @pl.when(some)
    def _():
        enter[:n] = eye
        enter[n:] = jnp.zeros((PAD, n), jnp.float32)
        for r in reversed(range(rounds)):

            @pl.when(takes(r))
            def _():
                @pl.when(jnp.logical_not(gathers(r)))
                def _():
                    map_copy(r, me, 0).wait_recv()

                enter[...] = compose(enter[...], got[r])

        start = enter[...]
        for k in reversed(range(slots)):
            keep(k, compose(start, maps[k]))

    def vec_copy(group, to):
        return pltpu.make_async_remote_copy(
            src_ref=vec_out,
            dst_ref=vec_in,
            send_sem=vec_send.at[to],
            recv_sem=vec_recv,
            device_id=(group, to),
            device_id_type=MESH,
        )

    @pl.when(place == 0)
    def _():
        vec_in[...] = eight(gap[...])

    @pl.when(place > 0)
    def _():
        vec_copy(seg, 0).wait_recv()

    stacked = jnp.concatenate(halves(vec_in[...]), axis=0).astype(jnp.bfloat16)

    def after(k):
        rows = jnp.dot(stacked, full[k], preferred_element_type=jnp.float32)
        rows = rows[:, :n] + rows[:, n:]
        return rows[:PAD] + rows[PAD:] + tails[k]

    @pl.when(passes_on)
    def _():
        vec_out[...] = after(slots - 1)
        for to in range(blocks - 1, -1, -1):
            vec_copy(seg + 1, to).start()

    for r in range(rounds):

        @pl.when(place == (1 << r) - 1)
        def _():
            vec_out[...] = after(slots - 1)
            for j in range(1 << r, 0, -1):
                vec_copy(seg, me + j).start()

    for k in range(slots):
        out_ref[0, k : k + 1] = jnp.where(live[k], nexts[k] + after(k)[0:1], 0.0)

    @pl.when(place > 0)
    def _():
        first_copy.wait_send()

    for r in range(rounds):

        @pl.when(gives(r))
        def _():
            for j in range(1 << r, 0, -1):
                map_copy(r, me + j, j - 1).wait_send()

        @pl.when(place == (1 << r) - 1)
        def _():
            for j in range(1 << r, 0, -1):
                vec_copy(seg, me + j).wait_send()

    @pl.when(passes_on)
    def _():
        for to in range(blocks):
            vec_copy(seg + 1, to).wait_send()


def body(
    jacobian,
    implicit_inv,
    input_map,
    controls,
    control_step,
    state_traj,
    terminal,
    init_gap,
    counts,
):
    segs, blocks = lax.axis_size("seg"), lax.axis_size("block")
    slots, n = state_traj.shape
    rounds = blocks.bit_length() - 1
    if blocks < 4 or blocks != 1 << rounds:
        raise ValueError("blocks")
    f32 = jnp.float32
    operands = (
        jacobian,
        implicit_inv,
        jnp.swapaxes(input_map, 1, 2),
        controls,
        control_step,
        state_traj,
        terminal[None],
        init_gap[None],
        counts,
    )
    out = pl.pallas_call(
        functools.partial(kernel, segs, blocks, rounds),
        out_shape=jax.ShapeDtypeStruct((2, slots, n), f32),
        in_specs=[pl.BlockSpec(memory_space=pltpu.HBM)] * len(operands),
        out_specs=pl.BlockSpec(memory_space=pltpu.VMEM),
        scratch_shapes=[pltpu.VMEM(x.shape, f32) for x in operands[:-1]]
        + [
            pltpu.SMEM(counts.shape, jnp.int32),
            pltpu.VMEM((1, n), f32),
            pltpu.VMEM((n + PAD, n), f32),
            pltpu.VMEM((rounds, n + PAD, n), f32),
            pltpu.VMEM((n + PAD, n), f32),
            pltpu.VMEM((slots, n + PAD, n), f32),
            pltpu.VMEM((slots, n, 2 * n), jnp.bfloat16),
            pltpu.VMEM((slots, PAD, n), f32),
            pltpu.VMEM((PAD, n), f32),
            pltpu.VMEM((PAD, n), f32),
            pltpu.SemaphoreType.DMA((len(operands),)),
            pltpu.SemaphoreType.DMA((2,)),
            pltpu.SemaphoreType.DMA((blocks,)),
            pltpu.SemaphoreType.DMA((rounds,)),
            pltpu.SemaphoreType.DMA((blocks,)),
            pltpu.SemaphoreType.DMA,
        ],
        compiler_params=pltpu.CompilerParams(
            collective_id=0, has_side_effects=True, vmem_limit_bytes=60 * 1024 * 1024
        ),
    )(*operands)
    return out[0], out[1]


def solution(mesh):
    in_specs = (
        P(("seg", "block"), None, None),
        P(("seg", "block"), None, None),
        P(("seg", "block"), None, None),
        P(("seg", "block"), None),
        P(("seg", "block"), None),
        P(("seg", "block"), None),
        P(),
        P(),
        P(("seg", "block")),
    )
    out_specs = (P(("seg", "block"), None), P(("seg", "block"), None))
    return jax.shard_map(body, mesh=mesh, in_specs=in_specs, out_specs=out_specs, check_vma=False)
```

```python
import functools
import jax
import jax.numpy as jnp
from jax import lax
from jax.experimental import pallas as pl
from jax.experimental.pallas import tpu as pltpu
from jax.sharding import PartitionSpec as P

MESH = pl.DeviceIdType.MESH
PAD = 8


def halves(x):
    high = x.astype(jnp.bfloat16).astype(jnp.float32)
    return high, x - high


def parts(x):
    if isinstance(x, tuple):
        return x
    return tuple(h.astype(jnp.bfloat16) for h in halves(x))


def product(left, right, turned):
    dims = (((1,), (1 if turned else 0,)), ((), ()))
    lh, ll = parts(left)
    rh, rl = parts(right)
    rows = jnp.concatenate([lh, ll], axis=1)
    if turned:
        other = jnp.concatenate([rh, rl], axis=0)
        other = jnp.concatenate([other, other], axis=1)
    else:
        other = jnp.concatenate([rh, rl], axis=1)
        other = jnp.concatenate([other, other], axis=0)
    out = lax.dot_general(rows, other, dims, preferred_element_type=jnp.float32)
    width = out.shape[1] // 2
    return out[:, :width] + out[:, width:]


def apply(rows, right, turned):
    count = rows.shape[0]
    dims = (((1,), (1 if turned else 0,)), ((), ()))
    stacked = jnp.concatenate(halves(rows), axis=0).astype(jnp.bfloat16)
    rh, rl = parts(right)
    other = jnp.concatenate([rh, rl], axis=0 if turned else 1)
    out = lax.dot_general(stacked, other, dims, preferred_element_type=jnp.float32)
    width = out.shape[1] // 2
    out = out[:, :width] + out[:, width:]
    return out[:count] + out[count:]


def compose(early, late):
    n = late.shape[1]
    zeros = jnp.zeros((PAD, n), jnp.float32)
    rows = product(jnp.concatenate([early, zeros], axis=0), late[:n], False)
    tail = rows[n : n + PAD] + late[n:]
    return jnp.concatenate([rows[:n], tail], axis=0)


def kernel(
    segs,
    blocks,
    rounds,
    jac_hbm,
    inv_hbm,
    inp_hbm,
    ctl_hbm,
    step_hbm,
    traj_hbm,
    term_hbm,
    gap_hbm,
    count_hbm,
    out_ref,
    jac,
    inv,
    inp,
    ctl,
    step,
    traj,
    term,
    gap,
    count,
    first,
    acc,
    got,
    enter,
    maps,
    full,
    tails,
    vec_in,
    vec_out,
    load_sem,
    first_sem,
    map_send,
    map_recv,
    vec_send,
    vec_recv,
):
    slots, n = traj.shape
    seg = lax.axis_index("seg")
    me = lax.axis_index("block")
    place = seg * blocks + me
    last = segs * blocks - 1
    passes_on = jnp.logical_and(me == blocks - 1, seg + 1 < segs)

    loads = [
        pltpu.make_async_copy(src, dst, load_sem.at[i])
        for i, (src, dst) in enumerate(
            (
                (traj_hbm, traj),
                (count_hbm, count),
                (jac_hbm, jac),
                (inv_hbm, inv),
                (inp_hbm, inp),
                (ctl_hbm, ctl),
                (step_hbm, step),
                (term_hbm, term),
                (gap_hbm, gap),
            )
        )
    ]
    barrier = pltpu.get_barrier_semaphore()

    def tell(s, b):
        pl.semaphore_signal(barrier, inc=1, device_id=(s, b), device_id_type=MESH)

    @pl.when(place < last)
    def _():
        tell((place + 1) // blocks, (place + 1) % blocks)

    peers = jnp.where(place > 0, 1, 0)
    for r in range(rounds):
        half = 1 << r

        @pl.when((me // half) % 2 == 1)
        def _():
            tell(seg, (me // half) * half - 1)

        peers += jnp.where(me % (2 * half) == half - 1, half, 0)

    @pl.when(seg > 0)
    def _():
        tell(seg - 1, blocks - 1)

    peers += jnp.where(passes_on, blocks, 0)
    for load in loads:
        load.start()
    pl.semaphore_wait(barrier, peers)

    ahead = jnp.maximum(place - 1, 0)
    first_copy = pltpu.make_async_remote_copy(
        src_ref=traj.at[pl.ds(0, 1)],
        dst_ref=first,
        send_sem=first_sem.at[0],
        recv_sem=first_sem.at[1],
        device_id=(ahead // blocks, ahead % blocks),
        device_id_type=MESH,
    )
    loads[0].wait()

    @pl.when(place > 0)
    def _():
        first_copy.start()

    row = lax.broadcasted_iota(jnp.int32, (n, n), 0)
    col = lax.broadcasted_iota(jnp.int32, (n, n), 1)
    eye = jnp.where(row == col, 1.0, 0.0).astype(jnp.float32)
    for load in loads[1:]:
        load.wait()
    live = [k < count[0] for k in range(slots)]

    jacs = [parts(jac[k]) for k in range(slots)]
    invs = [parts(inv[k]) for k in range(slots)]
    trans = [
        eye + jnp.where(live[k], product(invs[k], jacs[k], False), 0.0) for k in range(slots)
    ]
    steps = [parts(t) for t in trans]
    known = {}

    def fold(lo, hi):
        if (lo, hi) not in known:
            if hi - lo == 1:
                known[lo, hi] = trans[lo].T
            else:
                mid = (lo + hi) // 2 if lo or hi == slots else hi - 1
                early = fold(lo, mid)
                if hi - mid == 1:
                    known[lo, hi] = product(early, steps[mid], True)
                else:
                    known[lo, hi] = product(early, fold(mid, hi), False)
        return known[lo, hi]

    acc[:n] = fold(0, slots)
    for k in range(slots):
        maps[k, :n] = fold(0, k + 1)
    forced = []
    for k in range(slots):
        both = jnp.concatenate(
            [ctl[k : k + 1], step[k : k + 1], jnp.zeros((PAD - 2, ctl.shape[1]), jnp.float32)],
            axis=0,
        )
        forced.append(apply(both, inp[k], False))

    @pl.when(place < last)
    def _():
        first_copy.wait_recv()

    @pl.when(place == last)
    def _():
        first[...] = term[...]

    upcoming = first[...]

    def eight(x):
        return jnp.broadcast_to(x, (PAD, x.shape[1]))

    nexts, offsets = [], []
    for k in range(slots):
        now = traj[k : k + 1]
        if k + 1 < slots:
            nxt = jnp.where(live[k + 1], traj[k + 1 : k + 2], upcoming)
        else:
            nxt = upcoming
        nexts.append(nxt)
        change = eight(nxt - now)
        moved = forced[k]
        mid = apply(change, jacs[k], True) * (1.0 / 12.0) - eight(0.5 * (nxt + now))
        defect = change + apply(mid, jacs[k], True) - eight(moved[0:1])
        out_ref[1, k : k + 1] = jnp.where(live[k], defect[0:1], 0.0)
        offset = apply(eight(moved[1:2]) - defect, invs[k], True)
        offsets.append(jnp.where(live[k], offset, 0.0))
    known_vec = {}

    def fold_vec(lo, hi):
        if (lo, hi) not in known_vec:
            if hi - lo == 1:
                known_vec[lo, hi] = offsets[lo]
            else:
                mid = (lo + hi) // 2 if lo or hi == slots else hi - 1
                early = fold_vec(lo, mid)
                if hi - mid == 1:
                    moved = apply(early, steps[mid], True)
                else:
                    moved = apply(early, fold(mid, hi), False)
                known_vec[lo, hi] = moved + fold_vec(mid, hi)
        return known_vec[lo, hi]

    acc[n:] = fold_vec(0, slots)

    def at_front(r):
        return jnp.logical_and(seg == 0, me < (2 << r))

    def gives(r):
        half = 1 << r
        return jnp.logical_and(me % (2 * half) == half - 1, jnp.logical_not(at_front(r)))

    def gathers(r):
        half = 1 << r
        inner = jnp.logical_and(me % (2 * half) == 2 * half - 1, me < blocks - 1)
        return jnp.logical_and(inner, jnp.logical_not(at_front(r)))

    def takes(r):
        return jnp.logical_and((me // (1 << r)) % 2 == 1, jnp.logical_not(at_front(r)))

    def map_copy(r, to, j):
        return pltpu.make_async_remote_copy(
            src_ref=acc,
            dst_ref=got.at[r],
            send_sem=map_send.at[j],
            recv_sem=map_recv.at[r],
            device_id=(seg, to),
            device_id_type=MESH,
        )

    for r in range(rounds):

        @pl.when(gives(r))
        def _():
            for j in range(1 << r, 0, -1):
                map_copy(r, me + j, j - 1).start()

        @pl.when(gathers(r))
        def _():
            map_copy(r, me, 0).wait_recv()
            acc[...] = compose(got[r], acc[...])

    for k in range(slots):
        maps[k, n:] = fold_vec(0, k + 1)

    some = takes(0)
    for r in range(1, rounds):
        some = jnp.logical_or(some, takes(r))

    def keep(k, rows):
        full[k] = jnp.concatenate(halves(rows[:n]), axis=1).astype(jnp.bfloat16)
        tails[k] = rows[n:]

    @pl.when(jnp.logical_not(some))
    def _():
        for k in range(slots):
            keep(k, maps[k])

    @pl.when(some)
    def _():
        enter[:n] = eye
        enter[n:] = jnp.zeros((PAD, n), jnp.float32)
        for r in reversed(range(rounds)):

            @pl.when(takes(r))
            def _():
                @pl.when(jnp.logical_not(gathers(r)))
                def _():
                    map_copy(r, me, 0).wait_recv()

                enter[...] = compose(enter[...], got[r])

        start = enter[...]
        for k in reversed(range(slots)):
            keep(k, compose(start, maps[k]))

    def vec_copy(group, to):
        return pltpu.make_async_remote_copy(
            src_ref=vec_out,
            dst_ref=vec_in,
            send_sem=vec_send.at[to],
            recv_sem=vec_recv,
            device_id=(group, to),
            device_id_type=MESH,
        )

    @pl.when(place == 0)
    def _():
        vec_in[...] = eight(gap[...])

    @pl.when(place > 0)
    def _():
        vec_copy(seg, 0).wait_recv()

    stacked = jnp.concatenate(halves(vec_in[...]), axis=0).astype(jnp.bfloat16)

    def after(k):
        rows = jnp.dot(stacked, full[k], preferred_element_type=jnp.float32)
        rows = rows[:, :n] + rows[:, n:]
        return rows[:PAD] + rows[PAD:] + tails[k]

    @pl.when(passes_on)
    def _():
        vec_out[...] = after(slots - 1)
        for to in range(blocks - 1, -1, -1):
            vec_copy(seg + 1, to).start()

    for r in range(rounds):

        @pl.when(place == (1 << r) - 1)
        def _():
            vec_out[...] = after(slots - 1)
            for j in range(1 << r, 0, -1):
                vec_copy(seg, me + j).start()

    for k in range(slots):
        out_ref[0, k : k + 1] = jnp.where(live[k], nexts[k] + after(k)[0:1], 0.0)

    @pl.when(place > 0)
    def _():
        first_copy.wait_send()

    for r in range(rounds):

        @pl.when(gives(r))
        def _():
            for j in range(1 << r, 0, -1):
                map_copy(r, me + j, j - 1).wait_send()

        @pl.when(place == (1 << r) - 1)
        def _():
            for j in range(1 << r, 0, -1):
                vec_copy(seg, me + j).wait_send()

    @pl.when(passes_on)
    def _():
        for to in range(blocks):
            vec_copy(seg + 1, to).wait_send()


def body(
    jacobian,
    implicit_inv,
    input_map,
    controls,
    control_step,
    state_traj,
    terminal,
    init_gap,
    counts,
):
    segs, blocks = lax.axis_size("seg"), lax.axis_size("block")
    slots, n = state_traj.shape
    rounds = blocks.bit_length() - 1
    if blocks < 4 or blocks != 1 << rounds:
        raise ValueError("blocks")
    f32 = jnp.float32
    operands = (
        jacobian,
        implicit_inv,
        jnp.swapaxes(input_map, 1, 2),
        controls,
        control_step,
        state_traj,
        terminal[None],
        init_gap[None],
        counts,
    )
    out = pl.pallas_call(
        functools.partial(kernel, segs, blocks, rounds),
        out_shape=jax.ShapeDtypeStruct((2, slots, n), f32),
        in_specs=[pl.BlockSpec(memory_space=pltpu.HBM)] * len(operands),
        out_specs=pl.BlockSpec(memory_space=pltpu.VMEM),
        scratch_shapes=[pltpu.VMEM(x.shape, f32) for x in operands[:-1]]
        + [
            pltpu.SMEM(counts.shape, jnp.int32),
            pltpu.VMEM((1, n), f32),
            pltpu.VMEM((n + PAD, n), f32),
            pltpu.VMEM((rounds, n + PAD, n), f32),
            pltpu.VMEM((n + PAD, n), f32),
            pltpu.VMEM((slots, n + PAD, n), f32),
            pltpu.VMEM((slots, n, 2 * n), jnp.bfloat16),
            pltpu.VMEM((slots, PAD, n), f32),
            pltpu.VMEM((PAD, n), f32),
            pltpu.VMEM((PAD, n), f32),
            pltpu.SemaphoreType.DMA((len(operands),)),
            pltpu.SemaphoreType.DMA((2,)),
            pltpu.SemaphoreType.DMA((blocks,)),
            pltpu.SemaphoreType.DMA((rounds,)),
            pltpu.SemaphoreType.DMA((blocks,)),
            pltpu.SemaphoreType.DMA,
        ],
        compiler_params=pltpu.CompilerParams(
            collective_id=0, has_side_effects=True, vmem_limit_bytes=60 * 1024 * 1024
        ),
    )(*operands)
    return out[0], out[1]


def solution(mesh):
    in_specs = (
        P(("seg", "block"), None, None),
        P(("seg", "block"), None, None),
        P(("seg", "block"), None, None),
        P(("seg", "block"), None),
        P(("seg", "block"), None),
        P(("seg", "block"), None),
        P(),
        P(),
        P(("seg", "block")),
    )
    out_specs = (P(("seg", "block"), None), P(("seg", "block"), None))
    return jax.shard_map(body, mesh=mesh, in_specs=in_specs, out_specs=out_specs, check_vma=False)
```

```python
import functools
import jax
import jax.numpy as jnp
from jax import lax
from jax.experimental import pallas as pl
from jax.experimental.pallas import tpu as pltpu
from jax.sharding import PartitionSpec as P

MESH = pl.DeviceIdType.MESH
PAD = 8


def halves(x):
    high = x.astype(jnp.bfloat16).astype(jnp.float32)
    return high, x - high


def parts(x):
    if isinstance(x, tuple):
        return x
    return tuple(h.astype(jnp.bfloat16) for h in halves(x))


def product(left, right, turned):
    dims = (((1,), (1 if turned else 0,)), ((), ()))
    lh, ll = parts(left)
    rh, rl = parts(right)
    rows = jnp.concatenate([lh, ll], axis=1)
    if turned:
        other = jnp.concatenate([rh, rl], axis=0)
        other = jnp.concatenate([other, other], axis=1)
    else:
        other = jnp.concatenate([rh, rl], axis=1)
        other = jnp.concatenate([other, other], axis=0)
    out = lax.dot_general(rows, other, dims, preferred_element_type=jnp.float32)
    width = out.shape[1] // 2
    return out[:, :width] + out[:, width:]


def apply(rows, right, turned):
    count = rows.shape[0]
    dims = (((1,), (1 if turned else 0,)), ((), ()))
    stacked = jnp.concatenate(halves(rows), axis=0).astype(jnp.bfloat16)
    rh, rl = parts(right)
    other = jnp.concatenate([rh, rl], axis=0 if turned else 1)
    out = lax.dot_general(stacked, other, dims, preferred_element_type=jnp.float32)
    width = out.shape[1] // 2
    out = out[:, :width] + out[:, width:]
    return out[:count] + out[count:]


def compose(early, late):
    n = late.shape[1]
    zeros = jnp.zeros((PAD, n), jnp.float32)
    rows = product(jnp.concatenate([early, zeros], axis=0), late[:n], False)
    tail = rows[n : n + PAD] + late[n:]
    return jnp.concatenate([rows[:n], tail], axis=0)


def kernel(
    segs,
    blocks,
    rounds,
    jac_hbm,
    inv_hbm,
    inp_hbm,
    ctl_hbm,
    step_hbm,
    traj_hbm,
    term_hbm,
    gap_hbm,
    count_hbm,
    out_ref,
    jac,
    inv,
    inp,
    ctl,
    step,
    traj,
    term,
    gap,
    count,
    first,
    acc,
    got,
    enter,
    maps,
    full,
    tails,
    vec_in,
    vec_out,
    load_sem,
    first_sem,
    map_send,
    map_recv,
    vec_send,
    vec_recv,
):
    slots, n = traj.shape
    seg = lax.axis_index("seg")
    me = lax.axis_index("block")
    place = seg * blocks + me
    last = segs * blocks - 1
    passes_on = jnp.logical_and(me == blocks - 1, seg + 1 < segs)

    loads = [
        pltpu.make_async_copy(src, dst, load_sem.at[i])
        for i, (src, dst) in enumerate(
            (
                (traj_hbm, traj),
                (count_hbm, count),
                (jac_hbm, jac),
                (inv_hbm, inv),
                (inp_hbm, inp),
                (ctl_hbm, ctl),
                (step_hbm, step),
                (term_hbm, term),
                (gap_hbm, gap),
            )
        )
    ]
    barrier = pltpu.get_barrier_semaphore()

    def tell(s, b):
        pl.semaphore_signal(barrier, inc=1, device_id=(s, b), device_id_type=MESH)

    @pl.when(place < last)
    def _():
        tell((place + 1) // blocks, (place + 1) % blocks)

    peers = jnp.where(place > 0, 1, 0)
    for r in range(rounds):
        half = 1 << r

        @pl.when((me // half) % 2 == 1)
        def _():
            tell(seg, (me // half) * half - 1)

        peers += jnp.where(me % (2 * half) == half - 1, half, 0)

    @pl.when(seg > 0)
    def _():
        tell(seg - 1, blocks - 1)

    peers += jnp.where(passes_on, blocks, 0)
    for load in loads:
        load.start()
    pl.semaphore_wait(barrier, peers)

    ahead = jnp.maximum(place - 1, 0)
    first_copy = pltpu.make_async_remote_copy(
        src_ref=traj.at[pl.ds(0, 1)],
        dst_ref=first,
        send_sem=first_sem.at[0],
        recv_sem=first_sem.at[1],
        device_id=(ahead // blocks, ahead % blocks),
        device_id_type=MESH,
    )
    loads[0].wait()

    @pl.when(place > 0)
    def _():
        first_copy.start()

    row = lax.broadcasted_iota(jnp.int32, (n, n), 0)
    col = lax.broadcasted_iota(jnp.int32, (n, n), 1)
    eye = jnp.where(row == col, 1.0, 0.0).astype(jnp.float32)
    for load in loads[1:]:
        load.wait()
    live = [k < count[0] for k in range(slots)]

    jacs = [parts(jac[k]) for k in range(slots)]
    invs = [parts(inv[k]) for k in range(slots)]
    trans = [
        eye + jnp.where(live[k], product(invs[k], jacs[k], False), 0.0) for k in range(slots)
    ]
    steps = [parts(t) for t in trans]
    known = {}

    def fold(lo, hi):
        if (lo, hi) not in known:
            if hi - lo == 1:
                known[lo, hi] = trans[lo].T
            else:
                mid = (lo + hi) // 2 if lo or hi == slots else hi - 1
                early = fold(lo, mid)
                if hi - mid == 1:
                    known[lo, hi] = product(early, steps[mid], True)
                else:
                    known[lo, hi] = product(early, fold(mid, hi), False)
        return known[lo, hi]

    acc[:n] = fold(0, slots)
    for k in range(slots):
        maps[k, :n] = fold(0, k + 1)
    forced = []
    for k in range(slots):
        both = jnp.concatenate(
            [ctl[k : k + 1], step[k : k + 1], jnp.zeros((PAD - 2, ctl.shape[1]), jnp.float32)],
            axis=0,
        )
        forced.append(apply(both, inp[k], False))

    @pl.when(place < last)
    def _():
        first_copy.wait_recv()

    @pl.when(place == last)
    def _():
        first[...] = term[...]

    upcoming = first[...]

    def eight(x):
        return jnp.broadcast_to(x, (PAD, x.shape[1]))

    nexts, offsets = [], []
    for k in range(slots):
        now = traj[k : k + 1]
        if k + 1 < slots:
            nxt = jnp.where(live[k + 1], traj[k + 1 : k + 2], upcoming)
        else:
            nxt = upcoming
        nexts.append(nxt)
        change = eight(nxt - now)
        moved = forced[k]
        mid = apply(change, jacs[k], True) * (1.0 / 12.0) - eight(0.5 * (nxt + now))
        defect = change + apply(mid, jacs[k], True) - eight(moved[0:1])
        out_ref[1, k : k + 1] = jnp.where(live[k], defect[0:1], 0.0)
        offset = apply(eight(moved[1:2]) - defect, invs[k], True)
        offsets.append(jnp.where(live[k], offset, 0.0))
    known_vec = {}

    def fold_vec(lo, hi):
        if (lo, hi) not in known_vec:
            if hi - lo == 1:
                known_vec[lo, hi] = offsets[lo]
            else:
                mid = (lo + hi) // 2 if lo or hi == slots else hi - 1
                early = fold_vec(lo, mid)
                if hi - mid == 1:
                    moved = apply(early, steps[mid], True)
                else:
                    moved = apply(early, fold(mid, hi), False)
                known_vec[lo, hi] = moved + fold_vec(mid, hi)
        return known_vec[lo, hi]

    acc[n:] = fold_vec(0, slots)

    def at_front(r):
        return jnp.logical_and(seg == 0, me < (2 << r))

    def gives(r):
        half = 1 << r
        return jnp.logical_and(me % (2 * half) == half - 1, jnp.logical_not(at_front(r)))

    def gathers(r):
        half = 1 << r
        inner = jnp.logical_and(me % (2 * half) == 2 * half - 1, me < blocks - 1)
        return jnp.logical_and(inner, jnp.logical_not(at_front(r)))

    def takes(r):
        return jnp.logical_and((me // (1 << r)) % 2 == 1, jnp.logical_not(at_front(r)))

    def map_copy(r, to, j):
        return pltpu.make_async_remote_copy(
            src_ref=acc,
            dst_ref=got.at[r],
            send_sem=map_send.at[j],
            recv_sem=map_recv.at[r],
            device_id=(seg, to),
            device_id_type=MESH,
        )

    for r in range(rounds):

        @pl.when(gives(r))
        def _():
            for j in range(1 << r, 0, -1):
                map_copy(r, me + j, j - 1).start()

        @pl.when(gathers(r))
        def _():
            map_copy(r, me, 0).wait_recv()
            acc[...] = compose(got[r], acc[...])

    for k in range(slots):
        maps[k, n:] = fold_vec(0, k + 1)

    some = takes(0)
    for r in range(1, rounds):
        some = jnp.logical_or(some, takes(r))

    def keep(k, rows):
        full[k] = jnp.concatenate(halves(rows[:n]), axis=1).astype(jnp.bfloat16)
        tails[k] = rows[n:]

    @pl.when(jnp.logical_not(some))
    def _():
        for k in range(slots):
            keep(k, maps[k])

    @pl.when(some)
    def _():
        enter[:n] = eye
        enter[n:] = jnp.zeros((PAD, n), jnp.float32)
        for r in range(rounds):

            @pl.when(takes(r))
            def _():
                @pl.when(jnp.logical_not(gathers(r)))
                def _():
                    map_copy(r, me, 0).wait_recv()

                enter[...] = compose(got[r], enter[...])

        start = enter[...]
        for k in reversed(range(slots)):
            keep(k, compose(start, maps[k]))

    def vec_copy(group, to):
        return pltpu.make_async_remote_copy(
            src_ref=vec_out,
            dst_ref=vec_in,
            send_sem=vec_send.at[to],
            recv_sem=vec_recv,
            device_id=(group, to),
            device_id_type=MESH,
        )

    @pl.when(place == 0)
    def _():
        vec_in[...] = eight(gap[...])

    @pl.when(place > 0)
    def _():
        vec_copy(seg, 0).wait_recv()

    stacked = jnp.concatenate(halves(vec_in[...]), axis=0).astype(jnp.bfloat16)

    def after(k):
        rows = jnp.dot(stacked, full[k], preferred_element_type=jnp.float32)
        rows = rows[:, :n] + rows[:, n:]
        return rows[:PAD] + rows[PAD:] + tails[k]

    @pl.when(passes_on)
    def _():
        vec_out[...] = after(slots - 1)
        for to in range(blocks - 1, -1, -1):
            vec_copy(seg + 1, to).start()

    for r in range(rounds):

        @pl.when(place == (1 << r) - 1)
        def _():
            vec_out[...] = after(slots - 1)
            for j in range(1 << r, 0, -1):
                vec_copy(seg, me + j).start()

    for k in range(slots):
        out_ref[0, k : k + 1] = jnp.where(live[k], nexts[k] + after(k)[0:1], 0.0)

    @pl.when(place > 0)
    def _():
        first_copy.wait_send()

    for r in range(rounds):

        @pl.when(gives(r))
        def _():
            for j in range(1 << r, 0, -1):
                map_copy(r, me + j, j - 1).wait_send()

        @pl.when(place == (1 << r) - 1)
        def _():
            for j in range(1 << r, 0, -1):
                vec_copy(seg, me + j).wait_send()

    @pl.when(passes_on)
    def _():
        for to in range(blocks):
            vec_copy(seg + 1, to).wait_send()


def body(
    jacobian,
    implicit_inv,
    input_map,
    controls,
    control_step,
    state_traj,
    terminal,
    init_gap,
    counts,
):
    segs, blocks = lax.axis_size("seg"), lax.axis_size("block")
    slots, n = state_traj.shape
    rounds = blocks.bit_length() - 1
    if blocks < 4 or blocks != 1 << rounds:
        raise ValueError("blocks")
    f32 = jnp.float32
    operands = (
        jacobian,
        implicit_inv,
        jnp.swapaxes(input_map, 1, 2),
        controls,
        control_step,
        state_traj,
        terminal[None],
        init_gap[None],
        counts,
    )
    out = pl.pallas_call(
        functools.partial(kernel, segs, blocks, rounds),
        out_shape=jax.ShapeDtypeStruct((2, slots, n), f32),
        in_specs=[pl.BlockSpec(memory_space=pltpu.HBM)] * len(operands),
        out_specs=pl.BlockSpec(memory_space=pltpu.VMEM),
        scratch_shapes=[pltpu.VMEM(x.shape, f32) for x in operands[:-1]]
        + [
            pltpu.SMEM(counts.shape, jnp.int32),
            pltpu.VMEM((1, n), f32),
            pltpu.VMEM((n + PAD, n), f32),
            pltpu.VMEM((rounds, n + PAD, n), f32),
            pltpu.VMEM((n + PAD, n), f32),
            pltpu.VMEM((slots, n + PAD, n), f32),
            pltpu.VMEM((slots, n, 2 * n), jnp.bfloat16),
            pltpu.VMEM((slots, PAD, n), f32),
            pltpu.VMEM((PAD, n), f32),
            pltpu.VMEM((PAD, n), f32),
            pltpu.SemaphoreType.DMA((len(operands),)),
            pltpu.SemaphoreType.DMA((2,)),
            pltpu.SemaphoreType.DMA((blocks,)),
            pltpu.SemaphoreType.DMA((rounds,)),
            pltpu.SemaphoreType.DMA((blocks,)),
            pltpu.SemaphoreType.DMA,
        ],
        compiler_params=pltpu.CompilerParams(
            collective_id=0, has_side_effects=True, vmem_limit_bytes=60 * 1024 * 1024
        ),
    )(*operands)
    return out[0], out[1]


def solution(mesh):
    in_specs = (
        P(("seg", "block"), None, None),
        P(("seg", "block"), None, None),
        P(("seg", "block"), None, None),
        P(("seg", "block"), None),
        P(("seg", "block"), None),
        P(("seg", "block"), None),
        P(),
        P(),
        P(("seg", "block")),
    )
    out_specs = (P(("seg", "block"), None), P(("seg", "block"), None))
    return jax.shard_map(body, mesh=mesh, in_specs=in_specs, out_specs=out_specs, check_vma=False)
```
